32 devices in a mesh: wide: 8 (over y, x, core), narrow: 4 (over z).
Axes of the slice: x: 2, y: 2, z: 4, core: 2. Of those that a mesh axis runs over, the one named last changes fastest.
Arguments:
- tile_flow_speed: float32 [512, 3, 4096], P(('wide', 'narrow')), may hold values from -3 to 3
- tile_stress_mean: float32 [512, 4096], P(('wide', 'narrow')), may hold values from -3 to 3
- tile_heat_state: float32 [512, 4096], P(('wide', 'narrow')), may hold values from 0 to 1
- tile_drag_coefficient: float32 [512, 4096], P(('wide', 'narrow')), may hold values from 0.5 to 2
- marker_attributes: float32 [8, 262144], P(None, ('wide', 'narrow')), may hold values from -6 to 6
- marker_holding_tile: int32 [262144], P(('wide', 'narrow')), may hold values from 0 to 511, as said below
- marker_voxel_number: int32 [262144], P(('wide', 'narrow')), may hold values from 0 to 4095
- prior_slot_of_tile: int32 [512], P(('wide', 'narrow')), may hold values from 0 to 511, as said below
Outputs:
- velocity: float32 [3, 128, 128, 128], P(None, 'wide', 'narrow')
- pressure: float32 [128, 128, 128], P('wide', 'narrow')
- heat_on_fresh_grid: float32 [128, 128, 128], P('wide', 'narrow')
- bin_mean_attributes: float32 [8, 32, 32, 32], P(None, 'wide', 'narrow')
The draws below stay inside these ranges and needn't reach their ends.
Inputs may be any that keep to these rules, and one draw needn't show every extreme that they name: prior_slot_of_tile is a permutation: new owner q // 16 holds at place q % 16 the block that old owner prior_slot_of_tile[q] // 16 held at place prior_slot_of_tile[q] % 16. Every old owner sends to every new owner either none or exactly 1 of its blocks. `marker_holding_tile`: the tracer at position t is stored on old owner t // 8192 and lies in one of that owner's blocks. The tracers of one old owner whose blocks go to one new owner number at most 640, and every old owner has exactly 640 for one of its new owners.
All inputs are finite; a program needn't handle non-finite values.
Results may differ from the reference program's by a relative error of at most 0.00013.
Values sent between devices are 32-bit elements; how exact they have to be, the bound alone decides.
A program may use at most 256 MiB of HBM per device.

```python
import math
import jax
import jax.numpy as jnp

BS = 16
LX = 1
LY = 2
LZ = 8
TR_DEV = 8192
NPROP = 8
SWEEPS = 3
BLOCKS_DEV = 16
SUBGRID_COUNT = 512
SUBGRID_SITES = 4096
CAP = 1
GROUPS = 16
TCAP = 640
NT = 262144
NX = 128
NY = 128
NZ = 128
NXB = 32
NYB = 32
NZB = 32
N_WIDE = 8
N_NARROW = 4
DEVICES = 32


def draw_prior_slot_of_tile(key, part):
    base = jax.random.fold_in(key, 101)
    key_spread, key_shuffle, key_offset, key_places = jax.random.split(base, 4)
    spread = jax.random.permutation(key_spread, DEVICES)
    shuffle = jax.random.permutation(key_shuffle, DEVICES)
    offsets = jax.random.permutation(key_offset, DEVICES)
    device_ids = jnp.arange(DEVICES, dtype=jnp.int32)
    block_ids = jnp.arange(BLOCKS_DEV, dtype=jnp.int32)
    group_offset = offsets[block_ids // CAP]
    spread_inv = jnp.zeros((DEVICES,), jnp.int32).at[spread].set(device_ids)
    shuffle_inv = jnp.zeros((DEVICES,), jnp.int32).at[shuffle].set(device_ids)
    source = shuffle_inv[(spread_inv[device_ids][:, None] - group_offset[None, :]) % DEVICES]
    places = jax.vmap(lambda one_key: jax.random.permutation(one_key, BLOCKS_DEV))(jax.random.split(key_places, DEVICES))
    target = device_ids[:, None] * BLOCKS_DEV + places
    old_index = source * BLOCKS_DEV + block_ids[None, :]
    result = jnp.zeros((DEVICES * BLOCKS_DEV,), jnp.int32).at[target.reshape(-1)].set(old_index.reshape(-1))
    return result.astype(jnp.int32)


def draw_marker_holding_tile(key, part):
    base = jax.random.fold_in(key, 202)

    def one_source(source_key, source):
        key_full, key_caps, key_score, key_order, key_block = jax.random.split(source_key, 5)
        full_group = jax.random.randint(key_full, (), 0, GROUPS)
        group_ids = jnp.arange(GROUPS, dtype=jnp.int32)
        group_caps = jax.random.randint(key_caps, (GROUPS,), 4 * TCAP // 5, TCAP + 1)
        group_caps = jnp.where(group_ids == full_group, TCAP, group_caps)
        slot_total = GROUPS * TCAP
        slot_ids = jnp.arange(slot_total, dtype=jnp.int32)
        slot_group = slot_ids // TCAP
        slot_place = slot_ids % TCAP
        raw_score = jax.random.permutation(key_score, slot_total)
        score = jnp.where(slot_group == full_group, raw_score - slot_total, jnp.where(slot_place < group_caps[slot_group], raw_score, raw_score + slot_total))
        chosen = jnp.argsort(score, stable=True)[:TR_DEV]
        groups = (chosen // TCAP)[jax.random.permutation(key_order, TR_DEV)]
        local_block = groups * CAP + jax.random.randint(key_block, (TR_DEV,), 0, CAP)
        return source * BLOCKS_DEV + local_block
    keys = jax.random.split(base, DEVICES)
    result = jax.vmap(one_source)(keys, jnp.arange(DEVICES, dtype=jnp.int32))
    return result.reshape(-1).astype(jnp.int32)


def place_ends(array, own_key, smallest, high):
    dims = array.shape
    spot = [jax.random.randint(jax.random.fold_in(own_key, axis), (), 0, dims[axis]) for axis in range(len(dims))]
    array = array.at[tuple(spot)].set(smallest)
    longest = dims.index(max(dims))
    spot[longest] = (spot[longest] + 1) % dims[longest]
    return array.at[tuple(spot)].set(high)


def block_levels(key, extent, shards, smallest, high):
    level, own = 1.0, jax.random.fold_in(key, 6)
    for position, blocks in shards:
        heights = jnp.exp(jax.random.uniform(jax.random.fold_in(own, position), (blocks,), jnp.float32, smallest / len(shards), high / len(shards)))
        level = level * jnp.repeat(heights, extent[position] // blocks).reshape([-1 if axis == position else 1 for axis in range(len(extent))])
    return level


def gaussian(stream_key, dims, scale, limit, pieces=(), kind=jnp.bfloat16):
    values = scale * jax.random.normal(stream_key, dims, jnp.float32)
    if pieces:
        values = values * block_levels(stream_key, dims, pieces, -0.22, 0.18)
    return jnp.clip(values, -limit, limit).astype(kind)


def setup_inputs(seed: int = 0) -> dict:
    streams_of = jax.random.split(jax.random.key(seed), 9)
    return {
        "tile_flow_speed": gaussian(streams_of[0], (SUBGRID_COUNT, 3, SUBGRID_SITES), 0.5, 3.0, ((0, 32),), jnp.float32),
        "tile_stress_mean": gaussian(streams_of[1], (SUBGRID_COUNT, SUBGRID_SITES), 0.5, 3.0, ((0, 32),), jnp.float32),
        "tile_heat_state": jnp.clip(1.0 * jax.random.uniform(streams_of[2], (SUBGRID_COUNT, SUBGRID_SITES), jnp.float32) ** block_levels(streams_of[2], (SUBGRID_COUNT, SUBGRID_SITES), ((0, 32),), -0.2, 0.2), 0.0, 1.0),
        "tile_drag_coefficient": jnp.clip(jnp.exp(math.log(2.0) - 1.3862944 * jax.random.uniform(streams_of[3], (SUBGRID_COUNT, SUBGRID_SITES), jnp.float32) ** block_levels(streams_of[3], (SUBGRID_COUNT, SUBGRID_SITES), ((0, 32),), -0.2, 0.2)), 0.5, 2.0),
        "marker_attributes": gaussian(streams_of[4], (NPROP, NT), 1.0, 6.0, ((1, 32),), jnp.float32),
        "marker_holding_tile": draw_marker_holding_tile(jax.random.fold_in(streams_of[8], 71), 0),
        "marker_voxel_number": place_ends(jax.random.randint(streams_of[6], (NT,), 0, SUBGRID_SITES), jax.random.fold_in(streams_of[6], 1), 0, SUBGRID_SITES - 1).astype(jnp.int32),
        "prior_slot_of_tile": draw_prior_slot_of_tile(jax.random.fold_in(streams_of[8], 71), 0),
    }


MIX_WEIGHTS = (0.3, -0.25, 0.2, -0.15, 0.35, -0.3, 0.25, -0.2)
RELAX_WEIGHT = 0.7
PRESSURE_WEIGHT = 0.3
HEAT_FACTOR = 2.0
DENSITY_FACTOR = 4.0
DIRECTIONS = ((1, 0, 0), (-1, 0, 0), (0, 1, 0), (0, -1, 0), (0, 0, 1), (0, 0, -1))


def offset_view(field, shift):
    return field[1 + shift[0]:field.shape[0] - 1 + shift[0],
                 1 + shift[1]:field.shape[1] - 1 + shift[1],
                 1 + shift[2]:field.shape[2] - 1 + shift[2]]


def relax_sweep(state_pad, eta_pad, density_driving_term, hole):
    eta_centre = offset_view(eta_pad, (0, 0, 0))
    face_eta = [0.5 * (eta_centre + offset_view(eta_pad, shift)) for shift in DIRECTIONS]
    diagonal = face_eta[0]
    for index_m in range(1, 6):
        diagonal = diagonal + face_eta[index_m]
    diagonal = diagonal + hole
    press_pad = state_pad[3]
    updated = []
    divergence = None
    for component in range(3):
        speed_pad = state_pad[component]
        speed_centre = offset_view(speed_pad, (0, 0, 0))
        laplace = face_eta[0] * (offset_view(speed_pad, DIRECTIONS[0]) - speed_centre)
        for index_m in range(1, 6):
            laplace = laplace + face_eta[index_m] * (offset_view(speed_pad, DIRECTIONS[index_m]) - speed_centre)
        forward = DIRECTIONS[2 * component]
        backward = DIRECTIONS[2 * component + 1]
        gradient = 0.5 * (offset_view(press_pad, forward) - offset_view(press_pad, backward))
        residual = laplace - gradient
        if component == 2:
            residual = residual + density_driving_term
        updated.append(speed_centre + RELAX_WEIGHT * residual / diagonal)
        flux_term = 0.5 * (offset_view(speed_pad, forward) - offset_view(speed_pad, backward))
        divergence = flux_term if divergence is None else divergence + flux_term
    updated.append(offset_view(press_pad, (0, 0, 0)) - PRESSURE_WEIGHT * eta_centre * divergence)
    return jnp.stack(updated)


def spread_bins(field, edge):
    return jnp.repeat(jnp.repeat(jnp.repeat(field, edge, axis=0), edge, axis=1), edge, axis=2)


def reference(tile_flow_speed, tile_stress_mean, tile_heat_state, tile_drag_coefficient, marker_attributes, marker_holding_tile, marker_voxel_number, prior_slot_of_tile):
    def grid_arrangement(field):
        moved = field[prior_slot_of_tile]
        depth = field.shape[1]
        laid = moved.reshape(N_WIDE, N_NARROW, LX, LY, LZ, depth, BS, BS, BS)
        laid = laid.transpose(5, 0, 2, 6, 1, 3, 7, 4, 8)
        return laid.reshape(depth, NX, NY, NZ)

    velocity_start = grid_arrangement(tile_flow_speed)
    pressure_start = grid_arrangement(tile_stress_mean[:, None])[0]
    heat_on_fresh_grid = grid_arrangement(tile_heat_state[:, None])[0]
    reference_drag_level = grid_arrangement(tile_drag_coefficient[:, None])[0]

    inverse = jnp.zeros((SUBGRID_COUNT,), jnp.int32).at[prior_slot_of_tile].set(jnp.arange(SUBGRID_COUNT, dtype=jnp.int32))
    new_index = inverse[marker_holding_tile]
    owner = new_index // BLOCKS_DEV
    place = new_index % BLOCKS_DEV
    outer = owner // N_NARROW
    inner = owner % N_NARROW
    bin_edge = BS // 4
    layer = marker_voxel_number // (BS * BS)
    row_cell = (marker_voxel_number // BS) % BS
    column = marker_voxel_number % BS
    bin_x = (outer * LX + place // (LY * LZ)) * 4 + layer // bin_edge
    bin_y = (inner * LY + (place // LZ) % LY) * 4 + row_cell // bin_edge
    bin_z = (place % LZ) * 4 + column // bin_edge
    segment = ((bin_x * NYB + bin_y) * NZB + bin_z).astype(jnp.int32)
    bin_total = NXB * NYB * NZB
    prop_sums = jax.ops.segment_sum(marker_attributes.T, segment, bin_total)
    live_counts = jax.ops.segment_sum(jnp.ones((NT,), jnp.float32), segment, bin_total)
    bin_mean_attributes = prop_sums / jnp.maximum(live_counts, 1.0)[:, None]
    bin_mean_attributes = bin_mean_attributes.T.reshape(NPROP, NXB, NYB, NZB)

    mixture = MIX_WEIGHTS[0] * bin_mean_attributes[0]
    for index_p in range(1, NPROP):
        mixture = mixture + MIX_WEIGHTS[index_p] * bin_mean_attributes[index_p]
    voxel_blend_share = spread_bins(mixture, bin_edge)
    drag_coefficient_grid = reference_drag_level * jnp.exp(HEAT_FACTOR * (0.5 - heat_on_fresh_grid) + voxel_blend_share)
    density_driving_term = DENSITY_FACTOR * heat_on_fresh_grid

    solved_quantities = jnp.concatenate([velocity_start, pressure_start[None]], axis=0)
    eta_pad = jnp.pad(drag_coefficient_grid, 1)
    for sweep_step in range(SWEEPS):
        solved_quantities = relax_sweep(jnp.pad(solved_quantities, ((0, 0), (1, 1), (1, 1), (1, 1))), eta_pad, density_driving_term, 0.0)
    return solved_quantities[:3], solved_quantities[3], heat_on_fresh_grid, bin_mean_attributes
```

```python
import functools

import jax
import jax.numpy as jnp
from jax import lax
from jax.experimental import pallas as pl
from jax.experimental.pallas import tpu as pltpu
from jax.sharding import PartitionSpec as P

BS = 16
LX = 1
LY = 2
LZ = 8
SWEEPS = 3
BINS = 64

MIX_WEIGHTS = (0.3, -0.25, 0.2, -0.15, 0.35, -0.3, 0.25, -0.2)
RELAX_WEIGHT = 0.7
PRESSURE_WEIGHT = 0.3
HEAT_FACTOR = 2.0
DENSITY_FACTOR = 4.0
MESH = pl.DeviceIdType.MESH


def bin_kernel(base_ref, holder_ref, voxel_ref, attr_ref, mean_ref, *, blocks, chunk):
    props, tracers = attr_ref.shape
    total_bins = blocks * BINS
    base = base_ref[0]
    bin_ids = lax.broadcasted_iota(jnp.int32, (total_bins, chunk), 0)

    def step(turn, sums):
        at = pl.ds(pl.multiple_of(turn * chunk, chunk), chunk)
        voxel = voxel_ref[:, at]
        key = (
            (holder_ref[:, at] - base) * BINS
            + (voxel >> 10) * 16
            + ((voxel >> 6) & 3) * 4
            + ((voxel >> 2) & 3)
        )
        table = jnp.where(bin_ids == key, 1.0, 0.0).astype(jnp.bfloat16)
        values = attr_ref[:, at]
        high = values.astype(jnp.bfloat16)
        rest = values - high.astype(jnp.float32)
        middle = rest.astype(jnp.bfloat16)
        low = (rest - middle.astype(jnp.float32)).astype(jnp.bfloat16)
        ones = jnp.ones((props, chunk), jnp.bfloat16)
        rows = jnp.concatenate([high, middle, low, ones], axis=0)
        return sums + lax.dot_general(
            rows, table, (((1,), (1,)), ((), ())), preferred_element_type=jnp.float32
        )

    sums = lax.fori_loop(
        0, tracers // chunk, step, jnp.zeros((4 * props, total_bins), jnp.float32)
    )
    total = sums[:props] + sums[props : 2 * props] + sums[2 * props : 3 * props]
    mean_ref[...] = total / jnp.maximum(sums[3 * props :], 1.0)


def bin_means(base, holder, voxel, attributes, blocks):
    props, tracers = attributes.shape
    chunk = 1024 if tracers % 1024 == 0 else tracers
    vmem = pl.BlockSpec(memory_space=pltpu.VMEM)
    return pl.pallas_call(
        functools.partial(bin_kernel, blocks=blocks, chunk=chunk),
        out_shape=jax.ShapeDtypeStruct((props, blocks * BINS), jnp.float32),
        in_specs=[pl.BlockSpec(memory_space=pltpu.SMEM), vmem, vmem, vmem],
        out_specs=vmem,
        compiler_params=pltpu.CompilerParams(vmem_limit_bytes=32 * 1024 * 1024),
        cost_estimate=pl.CostEstimate(
            flops=2 * 32 * tracers * blocks * BINS, bytes_accessed=40 * tracers, transcendentals=0
        ),
    )(base.reshape(1), holder.reshape(1, tracers), voxel.reshape(1, tracers), attributes)


def swap_groups(x):
    row = lax.broadcasted_iota(jnp.int32, x.shape, 1)
    group = lax.broadcasted_iota(jnp.int32, x.shape, 2) // BS
    for bit in (1, 2, 4):
        row_set = (row & bit) != 0
        group_set = (group & bit) != 0
        from_above = pltpu.roll(pltpu.roll(x, 8 - bit, 1), BS * bit, 2)
        from_below = pltpu.roll(pltpu.roll(x, bit, 1), 8 * BS - BS * bit, 2)
        x = jnp.where(
            row_set == group_set, x, jnp.where(group_set, from_above, from_below)
        )
    return x


def pick_kernel(index_ref, from_ref, to_ref, sems):
    count = to_ref.shape[0]

    def copy_of(i):
        return pltpu.make_async_copy(from_ref.at[index_ref[i]], to_ref.at[i], sems.at[i])

    for i in range(count):
        copy_of(i).start()
    for i in range(count):
        copy_of(i).wait()


def pick(index, array):
    return pl.pallas_call(
        pick_kernel,
        out_shape=jax.ShapeDtypeStruct(index.shape + array.shape[1:], array.dtype),
        in_specs=[
            pl.BlockSpec(memory_space=pltpu.SMEM),
            pl.BlockSpec(memory_space=pl.ANY),
        ],
        out_specs=pl.BlockSpec(memory_space=pl.ANY),
        scratch_shapes=[pltpu.SemaphoreType.DMA(index.shape)],
    )(index, array)


def unpack_kernel(slot_ref, recv_ref, mix_ref, state_ref, heat_ref, held, sems):
    places = LY * LZ
    copies = []
    for r in range(places):
        copies.append(
            pltpu.make_async_copy(
                recv_ref.at[slot_ref[r]], held.at[r // LZ, :, r % LZ, :], sems.at[r]
            )
        )
        copies[-1].start()
    for copy in copies:
        copy.wait()
    spread = (
        lax.broadcasted_iota(jnp.int32, (32, 128), 0)
        == lax.broadcasted_iota(jnp.int32, (32, 128), 1) // 4
    ).astype(jnp.float32)
    wide_mix = jnp.dot(
        mix_ref[...], spread, precision=lax.Precision.HIGHEST, preferred_element_type=jnp.float32
    )
    for y in range(LY):
        rows = slice(y * BS, (y + 1) * BS)
        for field in range(4):
            part = swap_groups(held[y, field * 32 : (field + 1) * 32])
            state_ref[field, :, rows, :] = part.reshape(BS, BS, 128)
        heat = swap_groups(held[y, 128:160]).reshape(BS, BS, 128)
        heat_ref[:, rows, :] = heat
        drag = swap_groups(held[y, 160:192]).reshape(BS, BS, 128)
        for layer in range(4):
            piece = wide_mix[layer * 8 + y * 4 : layer * 8 + y * 4 + 4]
            piece = jnp.concatenate(
                [jnp.broadcast_to(piece[j : j + 1], (4, 128)) for j in range(4)], axis=0
            )
            at = slice(layer * 4, layer * 4 + 4)
            state_ref[4, at, rows, :] = drag[at] * jnp.exp(
                HEAT_FACTOR * (0.5 - heat[at]) + piece[None]
            )


def unpack(slots, received, mixture):
    grid_shape = (BS, LY * BS, LZ * BS)
    vmem = pl.BlockSpec(memory_space=pltpu.VMEM)
    return pl.pallas_call(
        unpack_kernel,
        out_shape=(
            jax.ShapeDtypeStruct((5,) + grid_shape, jnp.float32),
            jax.ShapeDtypeStruct(grid_shape, jnp.float32),
        ),
        in_specs=[
            pl.BlockSpec(memory_space=pltpu.SMEM),
            pl.BlockSpec(memory_space=pl.ANY),
            vmem,
        ],
        out_specs=(vmem, vmem),
        scratch_shapes=[
            pltpu.VMEM((LY, 192, LZ, 128), jnp.float32),
            pltpu.SemaphoreType.DMA((LY * LZ,)),
        ],
        compiler_params=pltpu.CompilerParams(vmem_limit_bytes=32 * 1024 * 1024),
    )(slots, received, mixture)


def sweep_kernel(
    state_ref, heat_ref, velocity_ref, pressure_ref,
    pad_0, pad_1, pad_2, edge_out, edge_in, send_sems, recv_sems,
    *, wide_count, narrow_count,
):
    wide, narrow = lax.axis_index("wide"), lax.axis_index("narrow")
    nx, ny, nz = heat_ref.shape
    exists = (wide > 0, wide < wide_count - 1, narrow > 0, narrow < narrow_count - 1)
    partner = ((wide - 1, narrow), (wide + 1, narrow), (wide, narrow - 1), (wide, narrow + 1))
    barrier = pltpu.get_barrier_semaphore()
    pads = (pad_0, pad_1, pad_2)
    for pad in pads:
        fields = pad.shape[0]
        for x in (0, nx + 1):
            pad[:, x] = jnp.zeros((fields, ny, nz), jnp.float32)
    edge_in[...] = jnp.zeros(edge_in.shape, jnp.float32)
    for side in range(4):

        @pl.when(exists[side])
        def _(side=side):
            pl.semaphore_signal(barrier, inc=1, device_id=partner[side], device_id_type=MESH)

    pad_0[:, 1 : nx + 1] = state_ref[...]
    pl.semaphore_wait(barrier, sum(there.astype(jnp.int32) for there in exists))

    row = lax.broadcasted_iota(jnp.int32, (ny, nz), 0)
    column = lax.broadcasted_iota(jnp.int32, (ny, nz), 1)

    def copy_of(turn, side):
        pad = pads[turn]
        fields = pad.shape[0]
        if side == 0:
            source, target = pad.at[:, 1], pad.at[:, nx + 1]
        elif side == 1:
            source, target = pad.at[:, nx], pad.at[:, 0]
        else:
            source = edge_out.at[turn, side - 2, pl.ds(0, fields)]
            target = edge_in.at[turn, 3 - side, pl.ds(0, fields)]
        return pltpu.make_async_remote_copy(
            src_ref=source,
            dst_ref=target,
            send_sem=send_sems.at[turn, side],
            recv_sem=recv_sems.at[turn, side ^ 1],
            device_id=partner[side],
            device_id_type=MESH,
        )

    def arrival_of(turn, side):
        pad = pads[turn]
        fields = pad.shape[0]
        if side < 2:
            target = pad.at[:, 0 if side == 0 else nx + 1]
        else:
            target = edge_in.at[turn, side - 2, pl.ds(0, fields)]
        return pltpu.make_async_remote_copy(
            src_ref=target,
            dst_ref=target,
            send_sem=send_sems.at[turn, side],
            recv_sem=recv_sems.at[turn, side],
            device_id=partner[side],
            device_id_type=MESH,
        )

    for turn in range(SWEEPS):
        pad = pads[turn]
        for side in range(2):

            @pl.when(exists[side])
            def _(side=side):
                copy_of(turn, side).start()

        for field in range(pad.shape[0]):
            edge_out[turn, 0, field] = pad[field, 1 : nx + 1, 0, :]
            edge_out[turn, 1, field] = pad[field, 1 : nx + 1, ny - 1, :]
        for side in range(2, 4):

            @pl.when(exists[side])
            def _(side=side):
                copy_of(turn, side).start()

        for side in range(4):

            @pl.when(exists[side])
            def _(side=side):
                arrival_of(turn, side).wait_recv()

        def slab(x, carry, turn=turn, pad=pad):
            def around(ref, edges, field):
                centre = ref[field, x + 1]
                low = edges[0, field, pl.ds(x, 1), :]
                high = edges[1, field, pl.ds(x, 1), :]
                return (
                    centre,
                    ref[field, x + 2],
                    ref[field, x],
                    jnp.where(row == ny - 1, high, pltpu.roll(centre, ny - 1, 0)),
                    jnp.where(row == 0, low, pltpu.roll(centre, 1, 0)),
                    jnp.where(column == nz - 1, 0.0, pltpu.roll(centre, nz - 1, 1)),
                    jnp.where(column == 0, 0.0, pltpu.roll(centre, 1, 1)),
                )

            eta = around(pad_0, edge_in.at[0], 4)
            face = [0.5 * (eta[0] + eta[m]) for m in range(1, 7)]
            diagonal = face[0]
            for m in range(1, 6):
                diagonal = diagonal + face[m]
            scale = RELAX_WEIGHT / diagonal
            press = around(pad, edge_in.at[turn], 3)
            divergence = None
            for component in range(3):
                speed = around(pad, edge_in.at[turn], component)
                residual = face[0] * (speed[1] - speed[0])
                for m in range(1, 6):
                    residual = residual + face[m] * (speed[m + 1] - speed[0])
                up, down = 2 * component + 1, 2 * component + 2
                residual = residual - 0.5 * (press[up] - press[down])
                if component == 2:
                    residual = residual + DENSITY_FACTOR * heat_ref[x]
                moved = speed[0] + residual * scale
                if turn < SWEEPS - 1:
                    pads[turn + 1][component, x + 1] = moved
                else:
                    velocity_ref[component, x] = moved
                flux = 0.5 * (speed[up] - speed[down])
                divergence = flux if divergence is None else divergence + flux
            moved = press[0] - PRESSURE_WEIGHT * eta[0] * divergence
            if turn < SWEEPS - 1:
                pads[turn + 1][3, x + 1] = moved
            else:
                pressure_ref[x] = moved
            return carry

        lax.fori_loop(0, nx, slab, 0)

    for turn in range(SWEEPS):
        for side in range(4):

            @pl.when(exists[side])
            def _(turn=turn, side=side):
                copy_of(turn, side).wait_send()


def sweeps(state, heat):
    nx, ny, nz = heat.shape
    vmem = pl.BlockSpec(memory_space=pltpu.VMEM)
    return pl.pallas_call(
        functools.partial(
            sweep_kernel,
            wide_count=lax.axis_size("wide"),
            narrow_count=lax.axis_size("narrow"),
        ),
        out_shape=(
            jax.ShapeDtypeStruct((3, nx, ny, nz), jnp.float32),
            jax.ShapeDtypeStruct((nx, ny, nz), jnp.float32),
        ),
        in_specs=[vmem, vmem],
        out_specs=(vmem, vmem),
        scratch_shapes=[
            pltpu.VMEM((5, nx + 2, ny, nz), jnp.float32),
            pltpu.VMEM((4, nx + 2, ny, nz), jnp.float32),
            pltpu.VMEM((4, nx + 2, ny, nz), jnp.float32),
            pltpu.VMEM((SWEEPS, 2, 5, nx, nz), jnp.float32),
            pltpu.VMEM((SWEEPS, 2, 5, nx, nz), jnp.float32),
            pltpu.SemaphoreType.DMA((SWEEPS, 4)),
            pltpu.SemaphoreType.DMA((SWEEPS, 4)),
        ],
        compiler_params=pltpu.CompilerParams(
            collective_id=1, has_side_effects=True, vmem_limit_bytes=32 * 1024 * 1024
        ),
    )(state, heat)


def per_device(
    tile_flow_speed,
    tile_stress_mean,
    tile_heat_state,
    tile_drag_coefficient,
    marker_attributes,
    marker_holding_tile,
    marker_voxel_number,
    prior_slot_of_tile,
):
    wide_count = lax.axis_size("wide")
    narrow_count = lax.axis_size("narrow")
    device_count = wide_count * narrow_count
    my_index = lax.axis_index("wide") * narrow_count + lax.axis_index("narrow")
    blocks = prior_slot_of_tile.shape[0]
    props = marker_attributes.shape[0]
    everything = lax.all_gather(prior_slot_of_tile, ("wide", "narrow"), axis=0, tiled=True)
    local_old = everything.reshape(device_count, blocks) - my_index * blocks
    is_mine = (local_old >= 0) & (local_old < blocks)
    block_for = jnp.sum(jnp.where(is_mine, local_old, 0), axis=1)
    stacked = jnp.concatenate(
        [
            tile_flow_speed.reshape(blocks, 96, 128),
            tile_stress_mean.reshape(blocks, 32, 128),
            tile_heat_state.reshape(blocks, 32, 128),
            tile_drag_coefficient.reshape(blocks, 32, 128),
        ],
        axis=1,
    )
    received = lax.all_to_all(
        pick(block_for, stacked), ("wide", "narrow"), split_axis=0, concat_axis=0, tiled=True
    )
    means = bin_means(
        my_index * blocks, marker_holding_tile, marker_voxel_number, marker_attributes, blocks
    )
    by_block = means.reshape(props, blocks, BINS).transpose(1, 0, 2).reshape(blocks, 4, 128)
    received_means = lax.all_to_all(
        pick(block_for, by_block), ("wide", "narrow"), split_axis=0, concat_axis=0, tiled=True
    )
    source_dev = prior_slot_of_tile // blocks
    arrived = pick(source_dev, received_means).reshape(LX, LY, LZ, props, 4, 4, 4)
    bin_mean_attributes = arrived.transpose(3, 0, 4, 1, 5, 2, 6)
    bin_mean_attributes = bin_mean_attributes.reshape(props, LX * 4, LY * 4, LZ * 4)
    mixture = MIX_WEIGHTS[0] * bin_mean_attributes[0]
    for index_p in range(1, props):
        mixture = mixture + MIX_WEIGHTS[index_p] * bin_mean_attributes[index_p]
    state, heat = unpack(source_dev, received, mixture.reshape(LY * BS, LZ * 4))
    velocity, pressure = sweeps(state, heat)
    return (velocity, pressure, heat, bin_mean_attributes)


def solution(mesh):
    in_specs = (
        P(("wide", "narrow"), None, None),
        P(("wide", "narrow"), None),
        P(("wide", "narrow"), None),
        P(("wide", "narrow"), None),
        P(None, ("wide", "narrow")),
        P(("wide", "narrow")),
        P(("wide", "narrow")),
        P(("wide", "narrow")),
    )
    out_specs = (
        P(None, "wide", "narrow", None),
        P("wide", "narrow", None),
        P("wide", "narrow", None),
        P(None, "wide", "narrow", None),
    )
    return jax.shard_map(
        per_device, mesh=mesh, in_specs=in_specs, out_specs=out_specs, check_vma=False
    )
```

```python
import functools

import jax
import jax.numpy as jnp
from jax import lax
from jax.experimental import pallas as pl
from jax.experimental.pallas import tpu as pltpu
from jax.sharding import PartitionSpec as P

BS = 16
LX = 1
LY = 2
LZ = 8
SWEEPS = 3
BINS = 64

MIX_WEIGHTS = (0.3, -0.25, 0.2, -0.15, 0.35, -0.3, 0.25, -0.2)
RELAX_WEIGHT = 0.7
PRESSURE_WEIGHT = 0.3
HEAT_FACTOR = 2.0
DENSITY_FACTOR = 4.0
MESH = pl.DeviceIdType.MESH


def choose_kernel(
    mine_ref, block_ref, table, send_sems, recv_sems, *, wide_count, narrow_count, blocks
):
    count = wide_count * narrow_count
    me = lax.axis_index("wide") * narrow_count + lax.axis_index("narrow")

    def place(step):
        return lax.rem(me + step, count)

    def coordinates(step):
        other = place(step)
        return (lax.div(other, narrow_count), lax.rem(other, narrow_count))

    barrier = pltpu.get_barrier_semaphore()

    def greet(step, carry):
        pl.semaphore_signal(barrier, inc=1, device_id=coordinates(step), device_id_type=MESH)
        return carry

    lax.fori_loop(1, count, greet, 0)
    pl.semaphore_wait(barrier, count - 1)

    def copy_of(step, target):
        return pltpu.make_async_remote_copy(
            src_ref=mine_ref.at[0],
            dst_ref=table.at[target],
            send_sem=send_sems.at[step],
            recv_sem=recv_sems.at[step],
            device_id=coordinates(step),
            device_id_type=MESH,
        )

    def send(step, carry):
        copy_of(step, me).start()
        return carry

    lax.fori_loop(1, count, send, 0)
    table[me] = mine_ref[0]

    def finish(step, carry):
        copy_of(step, place(count - step)).wait_recv()
        copy_of(step, me).wait_send()
        return carry

    lax.fori_loop(1, count, finish, 0)
    local_old = table[...] - me * blocks
    is_mine = (local_old >= 0) & (local_old < blocks)
    block_ref[...] = jnp.sum(jnp.where(is_mine, local_old, 0), axis=2)


def choose_blocks(prior_slots):
    wide_count, narrow_count = lax.axis_size("wide"), lax.axis_size("narrow")
    count, blocks = wide_count * narrow_count, prior_slots.shape[0]
    padded = jnp.pad(prior_slots, (0, 128 - blocks), constant_values=-1).reshape(1, 1, 128)
    vmem = pl.BlockSpec(memory_space=pltpu.VMEM)
    return pl.pallas_call(
        functools.partial(
            choose_kernel, wide_count=wide_count, narrow_count=narrow_count, blocks=blocks
        ),
        out_shape=jax.ShapeDtypeStruct((count, 1), jnp.int32),
        in_specs=[vmem],
        out_specs=vmem,
        scratch_shapes=[
            pltpu.VMEM((count, 1, 128), jnp.int32),
            pltpu.SemaphoreType.DMA((count,)),
            pltpu.SemaphoreType.DMA((count,)),
        ],
        compiler_params=pltpu.CompilerParams(collective_id=2, has_side_effects=True),
    )(padded).reshape(count)


def bin_kernel(base_ref, holder_ref, voxel_ref, attr_ref, mean_ref, *, blocks, chunk):
    props, tracers = attr_ref.shape
    total_bins = blocks * BINS
    base = base_ref[0]
    bin_ids = lax.broadcasted_iota(jnp.int32, (total_bins, chunk), 0)

    def step(turn, sums):
        at = pl.ds(pl.multiple_of(turn * chunk, chunk), chunk)
        voxel = voxel_ref[:, at]
        key = (
            (holder_ref[:, at] - base) * BINS
            + (voxel >> 10) * 16
            + ((voxel >> 6) & 3) * 4
            + ((voxel >> 2) & 3)
        )
        table = jnp.where(bin_ids == key, 1.0, 0.0).astype(jnp.bfloat16)
        values = attr_ref[:, at]
        high = values.astype(jnp.bfloat16)
        rest = values - high.astype(jnp.float32)
        middle = rest.astype(jnp.bfloat16)
        low = (rest - middle.astype(jnp.float32)).astype(jnp.bfloat16)
        ones = jnp.ones((props, chunk), jnp.bfloat16)
        rows = jnp.concatenate([high, middle, low, ones], axis=0)
        return sums + lax.dot_general(
            rows, table, (((1,), (1,)), ((), ())), preferred_element_type=jnp.float32
        )

    sums = lax.fori_loop(
        0, tracers // chunk, step, jnp.zeros((4 * props, total_bins), jnp.float32)
    )
    total = sums[:props] + sums[props : 2 * props] + sums[2 * props : 3 * props]
    mean_ref[...] = total / jnp.maximum(sums[3 * props :], 1.0)


def bin_means(base, holder, voxel, attributes, blocks):
    props, tracers = attributes.shape
    chunk = 1024 if tracers % 1024 == 0 else tracers
    vmem = pl.BlockSpec(memory_space=pltpu.VMEM)
    return pl.pallas_call(
        functools.partial(bin_kernel, blocks=blocks, chunk=chunk),
        out_shape=jax.ShapeDtypeStruct((props, blocks * BINS), jnp.float32),
        in_specs=[pl.BlockSpec(memory_space=pltpu.SMEM), vmem, vmem, vmem],
        out_specs=vmem,
        compiler_params=pltpu.CompilerParams(vmem_limit_bytes=32 * 1024 * 1024),
        cost_estimate=pl.CostEstimate(
            flops=2 * 32 * tracers * blocks * BINS, bytes_accessed=40 * tracers, transcendentals=0
        ),
    )(base.reshape(1), holder.reshape(1, tracers), voxel.reshape(1, tracers), attributes)


def swap_groups(x):
    row = lax.broadcasted_iota(jnp.int32, x.shape, 1)
    group = lax.broadcasted_iota(jnp.int32, x.shape, 2) // BS
    for bit in (1, 2, 4):
        row_set = (row & bit) != 0
        group_set = (group & bit) != 0
        from_above = pltpu.roll(pltpu.roll(x, 8 - bit, 1), BS * bit, 2)
        from_below = pltpu.roll(pltpu.roll(x, bit, 1), 8 * BS - BS * bit, 2)
        x = jnp.where(
            row_set == group_set, x, jnp.where(group_set, from_above, from_below)
        )
    return x


def pick_kernel(index_ref, from_ref, to_ref, sems):
    count = to_ref.shape[0]

    def copy_of(i):
        return pltpu.make_async_copy(from_ref.at[index_ref[i]], to_ref.at[i], sems.at[i])

    for i in range(count):
        copy_of(i).start()
    for i in range(count):
        copy_of(i).wait()


def pick(index, array):
    return pl.pallas_call(
        pick_kernel,
        out_shape=jax.ShapeDtypeStruct(index.shape + array.shape[1:], array.dtype),
        in_specs=[
            pl.BlockSpec(memory_space=pltpu.SMEM),
            pl.BlockSpec(memory_space=pltpu.VMEM),
        ],
        out_specs=pl.BlockSpec(memory_space=pl.ANY),
        scratch_shapes=[pltpu.SemaphoreType.DMA(index.shape)],
        compiler_params=pltpu.CompilerParams(vmem_limit_bytes=32 * 1024 * 1024),
    )(index, array)


def unpack_kernel(slot_ref, recv_ref, mix_ref, state_ref, heat_ref, held, sems):
    places = LY * LZ
    copies = []
    for r in range(places):
        copies.append(
            pltpu.make_async_copy(
                recv_ref.at[slot_ref[r]], held.at[r // LZ, :, r % LZ, :], sems.at[r]
            )
        )
        copies[-1].start()
    for copy in copies:
        copy.wait()
    spread = (
        lax.broadcasted_iota(jnp.int32, (32, 128), 0)
        == lax.broadcasted_iota(jnp.int32, (32, 128), 1) // 4
    ).astype(jnp.float32)
    wide_mix = jnp.dot(
        mix_ref[...], spread, precision=lax.Precision.HIGHEST, preferred_element_type=jnp.float32
    )
    for y in range(LY):
        rows = slice(y * BS, (y + 1) * BS)
        for field in range(4):
            part = swap_groups(held[y, field * 32 : (field + 1) * 32])
            state_ref[field, :, rows, :] = part.reshape(BS, BS, 128)
        heat = swap_groups(held[y, 128:160]).reshape(BS, BS, 128)
        heat_ref[:, rows, :] = heat
        drag = swap_groups(held[y, 160:192]).reshape(BS, BS, 128)
        for layer in range(4):
            piece = wide_mix[layer * 8 + y * 4 : layer * 8 + y * 4 + 4]
            piece = jnp.concatenate(
                [jnp.broadcast_to(piece[j : j + 1], (4, 128)) for j in range(4)], axis=0
            )
            at = slice(layer * 4, layer * 4 + 4)
            state_ref[4, at, rows, :] = drag[at] * jnp.exp(
                HEAT_FACTOR * (0.5 - heat[at]) + piece[None]
            )


def unpack(slots, received, mixture):
    grid_shape = (BS, LY * BS, LZ * BS)
    vmem = pl.BlockSpec(memory_space=pltpu.VMEM)
    return pl.pallas_call(
        unpack_kernel,
        out_shape=(
            jax.ShapeDtypeStruct((5,) + grid_shape, jnp.float32),
            jax.ShapeDtypeStruct(grid_shape, jnp.float32),
        ),
        in_specs=[
            pl.BlockSpec(memory_space=pltpu.SMEM),
            pl.BlockSpec(memory_space=pl.ANY),
            vmem,
        ],
        out_specs=(vmem, vmem),
        scratch_shapes=[
            pltpu.VMEM((LY, 192, LZ, 128), jnp.float32),
            pltpu.SemaphoreType.DMA((LY * LZ,)),
        ],
        compiler_params=pltpu.CompilerParams(vmem_limit_bytes=32 * 1024 * 1024),
    )(slots, received, mixture)


def sweep_kernel(
    state_ref, heat_ref, velocity_ref, pressure_ref,
    pad_0, pad_1, pad_2, edge_out, edge_in, send_sems, recv_sems,
    *, wide_count, narrow_count,
):
    wide, narrow = lax.axis_index("wide"), lax.axis_index("narrow")
    nx, ny, nz = heat_ref.shape
    exists = (wide > 0, wide < wide_count - 1, narrow > 0, narrow < narrow_count - 1)
    partner = ((wide - 1, narrow), (wide + 1, narrow), (wide, narrow - 1), (wide, narrow + 1))
    barrier = pltpu.get_barrier_semaphore()
    pads = (pad_0, pad_1, pad_2)
    for pad in pads:
        fields = pad.shape[0]
        for x in (0, nx + 1):
            pad[:, x] = jnp.zeros((fields, ny, nz), jnp.float32)
    edge_in[...] = jnp.zeros(edge_in.shape, jnp.float32)
    for side in range(4):

        @pl.when(exists[side])
        def _(side=side):
            pl.semaphore_signal(barrier, inc=1, device_id=partner[side], device_id_type=MESH)

    pad_0[:, 1 : nx + 1] = state_ref[...]
    pl.semaphore_wait(barrier, sum(there.astype(jnp.int32) for there in exists))

    row = lax.broadcasted_iota(jnp.int32, (ny, nz), 0)
    column = lax.broadcasted_iota(jnp.int32, (ny, nz), 1)

    def copy_of(turn, side):
        pad = pads[turn]
        fields = pad.shape[0]
        if side == 0:
            source, target = pad.at[:, 1], pad.at[:, nx + 1]
        elif side == 1:
            source, target = pad.at[:, nx], pad.at[:, 0]
        else:
            source = edge_out.at[turn, side - 2, pl.ds(0, fields)]
            target = edge_in.at[turn, 3 - side, pl.ds(0, fields)]
        return pltpu.make_async_remote_copy(
            src_ref=source,
            dst_ref=target,
            send_sem=send_sems.at[turn, side],
            recv_sem=recv_sems.at[turn, side ^ 1],
            device_id=partner[side],
            device_id_type=MESH,
        )

    def arrival_of(turn, side):
        pad = pads[turn]
        fields = pad.shape[0]
        if side < 2:
            target = pad.at[:, 0 if side == 0 else nx + 1]
        else:
            target = edge_in.at[turn, side - 2, pl.ds(0, fields)]
        return pltpu.make_async_remote_copy(
            src_ref=target,
            dst_ref=target,
            send_sem=send_sems.at[turn, side],
            recv_sem=recv_sems.at[turn, side],
            device_id=partner[side],
            device_id_type=MESH,
        )

    for turn in range(SWEEPS):
        pad = pads[turn]
        for side in range(2):

            @pl.when(exists[side])
            def _(side=side):
                copy_of(turn, side).start()

        for field in range(pad.shape[0]):
            edge_out[turn, 0, field] = pad[field, 1 : nx + 1, 0, :]
            edge_out[turn, 1, field] = pad[field, 1 : nx + 1, ny - 1, :]
        for side in range(2, 4):

            @pl.when(exists[side])
            def _(side=side):
                copy_of(turn, side).start()

        for side in range(4):

            @pl.when(exists[side])
            def _(side=side):
                arrival_of(turn, side).wait_recv()

        def slab(x, carry, turn=turn, pad=pad):
            def around(ref, edges, field):
                centre = ref[field, x + 1]
                low = edges[0, field, pl.ds(x, 1), :]
                high = edges[1, field, pl.ds(x, 1), :]
                return (
                    centre,
                    ref[field, x + 2],
                    ref[field, x],
                    jnp.where(row == ny - 1, high, pltpu.roll(centre, ny - 1, 0)),
                    jnp.where(row == 0, low, pltpu.roll(centre, 1, 0)),
                    jnp.where(column == nz - 1, 0.0, pltpu.roll(centre, nz - 1, 1)),
                    jnp.where(column == 0, 0.0, pltpu.roll(centre, 1, 1)),
                )

            eta = around(pad_0, edge_in.at[0], 4)
            face = [0.5 * (eta[0] + eta[m]) for m in range(1, 7)]
            diagonal = face[0]
            for m in range(1, 6):
                diagonal = diagonal + face[m]
            scale = RELAX_WEIGHT / diagonal
            press = around(pad, edge_in.at[turn], 3)
            divergence = None
            for component in range(3):
                speed = around(pad, edge_in.at[turn], component)
                residual = face[0] * (speed[1] - speed[0])
                for m in range(1, 6):
                    residual = residual + face[m] * (speed[m + 1] - speed[0])
                up, down = 2 * component + 1, 2 * component + 2
                residual = residual - 0.5 * (press[up] - press[down])
                if component == 2:
                    residual = residual + DENSITY_FACTOR * heat_ref[x]
                moved = speed[0] + residual * scale
                if turn < SWEEPS - 1:
                    pads[turn + 1][component, x + 1] = moved
                else:
                    velocity_ref[component, x] = moved
                flux = 0.5 * (speed[up] - speed[down])
                divergence = flux if divergence is None else divergence + flux
            moved = press[0] - PRESSURE_WEIGHT * eta[0] * divergence
            if turn < SWEEPS - 1:
                pads[turn + 1][3, x + 1] = moved
            else:
                pressure_ref[x] = moved
            return carry

        lax.fori_loop(0, nx, slab, 0)

    for turn in range(SWEEPS):
        for side in range(4):

            @pl.when(exists[side])
            def _(turn=turn, side=side):
                copy_of(turn, side).wait_send()


def sweeps(state, heat):
    nx, ny, nz = heat.shape
    vmem = pl.BlockSpec(memory_space=pltpu.VMEM)
    return pl.pallas_call(
        functools.partial(
            sweep_kernel,
            wide_count=lax.axis_size("wide"),
            narrow_count=lax.axis_size("narrow"),
        ),
        out_shape=(
            jax.ShapeDtypeStruct((3, nx, ny, nz), jnp.float32),
            jax.ShapeDtypeStruct((nx, ny, nz), jnp.float32),
        ),
        in_specs=[vmem, vmem],
        out_specs=(vmem, vmem),
        scratch_shapes=[
            pltpu.VMEM((5, nx + 2, ny, nz), jnp.float32),
            pltpu.VMEM((4, nx + 2, ny, nz), jnp.float32),
            pltpu.VMEM((4, nx + 2, ny, nz), jnp.float32),
            pltpu.VMEM((SWEEPS, 2, 5, nx, nz), jnp.float32),
            pltpu.VMEM((SWEEPS, 2, 5, nx, nz), jnp.float32),
            pltpu.SemaphoreType.DMA((SWEEPS, 4)),
            pltpu.SemaphoreType.DMA((SWEEPS, 4)),
        ],
        compiler_params=pltpu.CompilerParams(
            collective_id=1, has_side_effects=True, vmem_limit_bytes=32 * 1024 * 1024
        ),
    )(state, heat)


def per_device(
    tile_flow_speed,
    tile_stress_mean,
    tile_heat_state,
    tile_drag_coefficient,
    marker_attributes,
    marker_holding_tile,
    marker_voxel_number,
    prior_slot_of_tile,
):
    wide_count = lax.axis_size("wide")
    narrow_count = lax.axis_size("narrow")
    my_index = lax.axis_index("wide") * narrow_count + lax.axis_index("narrow")
    blocks = prior_slot_of_tile.shape[0]
    props = marker_attributes.shape[0]
    block_for = choose_blocks(prior_slot_of_tile)
    stacked = jnp.concatenate(
        [
            tile_flow_speed.reshape(blocks, 96, 128),
            tile_stress_mean.reshape(blocks, 32, 128),
            tile_heat_state.reshape(blocks, 32, 128),
            tile_drag_coefficient.reshape(blocks, 32, 128),
        ],
        axis=1,
    )
    outgoing = pick(block_for, stacked)
    outgoing, marker_attributes = lax.optimization_barrier((outgoing, marker_attributes))
    received = lax.all_to_all(
        outgoing, ("wide", "narrow"), split_axis=0, concat_axis=0, tiled=True
    )
    means = bin_means(
        my_index * blocks, marker_holding_tile, marker_voxel_number, marker_attributes, blocks
    )
    by_block = means.reshape(props, blocks, BINS).transpose(1, 0, 2).reshape(blocks, 4, 128)
    received_means = lax.all_to_all(
        pick(block_for, by_block), ("wide", "narrow"), split_axis=0, concat_axis=0, tiled=True
    )
    source_dev = prior_slot_of_tile // blocks
    arrived = pick(source_dev, received_means).reshape(LX, LY, LZ, props, 4, 4, 4)
    bin_mean_attributes = arrived.transpose(3, 0, 4, 1, 5, 2, 6)
    bin_mean_attributes = bin_mean_attributes.reshape(props, LX * 4, LY * 4, LZ * 4)
    mixture = MIX_WEIGHTS[0] * bin_mean_attributes[0]
    for index_p in range(1, props):
        mixture = mixture + MIX_WEIGHTS[index_p] * bin_mean_attributes[index_p]
    state, heat = unpack(source_dev, received, mixture.reshape(LY * BS, LZ * 4))
    velocity, pressure = sweeps(state, heat)
    return (velocity, pressure, heat, bin_mean_attributes)


def solution(mesh):
    in_specs = (
        P(("wide", "narrow"), None, None),
        P(("wide", "narrow"), None),
        P(("wide", "narrow"), None),
        P(("wide", "narrow"), None),
        P(None, ("wide", "narrow")),
        P(("wide", "narrow")),
        P(("wide", "narrow")),
        P(("wide", "narrow")),
    )
    out_specs = (
        P(None, "wide", "narrow", None),
        P("wide", "narrow", None),
        P("wide", "narrow", None),
        P(None, "wide", "narrow", None),
    )
    return jax.shard_map(
        per_device, mesh=mesh, in_specs=in_specs, out_specs=out_specs, check_vma=False
    )
```

```python
import functools

import jax
import jax.numpy as jnp
from jax import lax
from jax.experimental import pallas as pl
from jax.experimental.pallas import tpu as pltpu
from jax.sharding import PartitionSpec as P

BS = 16
LX = 1
LY = 2
LZ = 8
SWEEPS = 3
BINS = 64

MIX_WEIGHTS = (0.3, -0.25, 0.2, -0.15, 0.35, -0.3, 0.25, -0.2)
RELAX_WEIGHT = 0.7
PRESSURE_WEIGHT = 0.3
HEAT_FACTOR = 2.0
DENSITY_FACTOR = 4.0
MESH = pl.DeviceIdType.MESH


def choose_kernel(
    mine_ref, block_ref, table, send_sems, recv_sems, *, wide_count, narrow_count, blocks
):
    count = wide_count * narrow_count
    me = lax.axis_index("wide") * narrow_count + lax.axis_index("narrow")

    def place(step):
        return lax.rem(me + step, count)

    def coordinates(step):
        other = place(step)
        return (lax.div(other, narrow_count), lax.rem(other, narrow_count))

    barrier = pltpu.get_barrier_semaphore()

    def greet(step, carry):
        pl.semaphore_signal(barrier, inc=1, device_id=coordinates(step), device_id_type=MESH)
        return carry

    lax.fori_loop(1, count, greet, 0)
    pl.semaphore_wait(barrier, count - 1)

    def copy_of(step, target):
        return pltpu.make_async_remote_copy(
            src_ref=mine_ref.at[0],
            dst_ref=table.at[target],
            send_sem=send_sems.at[step],
            recv_sem=recv_sems.at[step],
            device_id=coordinates(step),
            device_id_type=MESH,
        )

    def send(step, carry):
        copy_of(step, me).start()
        return carry

    lax.fori_loop(1, count, send, 0)
    table[me] = mine_ref[0]

    def finish(step, carry):
        copy_of(step, place(count - step)).wait_recv()
        copy_of(step, me).wait_send()
        return carry

    lax.fori_loop(1, count, finish, 0)
    local_old = table[...] - me * blocks
    is_mine = (local_old >= 0) & (local_old < blocks)
    block_ref[...] = jnp.sum(jnp.where(is_mine, local_old, 0), axis=2)


def choose_blocks(prior_slots):
    wide_count, narrow_count = lax.axis_size("wide"), lax.axis_size("narrow")
    count, blocks = wide_count * narrow_count, prior_slots.shape[0]
    padded = jnp.pad(prior_slots, (0, 128 - blocks), constant_values=-1).reshape(1, 1, 128)
    vmem = pl.BlockSpec(memory_space=pltpu.VMEM)
    return pl.pallas_call(
        functools.partial(
            choose_kernel, wide_count=wide_count, narrow_count=narrow_count, blocks=blocks
        ),
        out_shape=jax.ShapeDtypeStruct((count, 1), jnp.int32),
        in_specs=[vmem],
        out_specs=vmem,
        scratch_shapes=[
            pltpu.VMEM((count, 1, 128), jnp.int32),
            pltpu.SemaphoreType.DMA((count,)),
            pltpu.SemaphoreType.DMA((count,)),
        ],
        compiler_params=pltpu.CompilerParams(collective_id=2, has_side_effects=True),
    )(padded).reshape(count)


def exchange_kernel(
    send_ref, out_ref, landed, send_sems, recv_sems, *, wide_count, narrow_count
):
    count = wide_count * narrow_count
    me = lax.axis_index("wide") * narrow_count + lax.axis_index("narrow")

    def place(step):
        return lax.rem(me + step, count)

    def coordinates(step):
        other = place(step)
        return (lax.div(other, narrow_count), lax.rem(other, narrow_count))

    barrier = pltpu.get_barrier_semaphore()

    def greet(step, carry):
        pl.semaphore_signal(barrier, inc=1, device_id=coordinates(step), device_id_type=MESH)
        return carry

    lax.fori_loop(1, count, greet, 0)
    pl.semaphore_wait(barrier, count - 1)

    def copy_of(step, target):
        return pltpu.make_async_remote_copy(
            src_ref=send_ref.at[place(step)],
            dst_ref=landed.at[target],
            send_sem=send_sems.at[step],
            recv_sem=recv_sems.at[step],
            device_id=coordinates(step),
            device_id_type=MESH,
        )

    def send(step, carry):
        copy_of(step, me).start()
        return carry

    lax.fori_loop(1, count, send, 0)
    landed[me] = send_ref[me]

    def finish(step, carry):
        copy_of(step, place(count - step)).wait_recv()
        copy_of(step, me).wait_send()
        return carry

    lax.fori_loop(1, count, finish, 0)
    out_ref[...] = landed[...]


def exchange(entries):
    wide_count, narrow_count = lax.axis_size("wide"), lax.axis_size("narrow")
    count = wide_count * narrow_count
    vmem = pl.BlockSpec(memory_space=pltpu.VMEM)
    return pl.pallas_call(
        functools.partial(exchange_kernel, wide_count=wide_count, narrow_count=narrow_count),
        out_shape=jax.ShapeDtypeStruct(entries.shape, entries.dtype),
        in_specs=[vmem],
        out_specs=vmem,
        scratch_shapes=[
            pltpu.VMEM(entries.shape, entries.dtype),
            pltpu.SemaphoreType.DMA((count,)),
            pltpu.SemaphoreType.DMA((count,)),
        ],
        compiler_params=pltpu.CompilerParams(
            collective_id=3, has_side_effects=True, vmem_limit_bytes=32 * 1024 * 1024
        ),
    )(entries)


def bin_kernel(base_ref, holder_ref, voxel_ref, attr_ref, mean_ref, *, blocks, chunk):
    props, tracers = attr_ref.shape
    total_bins = blocks * BINS
    base = base_ref[0]
    bin_ids = lax.broadcasted_iota(jnp.int32, (total_bins, chunk), 0)

    def step(turn, sums):
        at = pl.ds(pl.multiple_of(turn * chunk, chunk), chunk)
        voxel = voxel_ref[:, at]
        key = (
            (holder_ref[:, at] - base) * BINS
            + (voxel >> 10) * 16
            + ((voxel >> 6) & 3) * 4
            + ((voxel >> 2) & 3)
        )
        table = jnp.where(bin_ids == key, 1.0, 0.0).astype(jnp.bfloat16)
        values = attr_ref[:, at]
        high = values.astype(jnp.bfloat16)
        rest = values - high.astype(jnp.float32)
        middle = rest.astype(jnp.bfloat16)
        low = (rest - middle.astype(jnp.float32)).astype(jnp.bfloat16)
        ones = jnp.ones((props, chunk), jnp.bfloat16)
        rows = jnp.concatenate([high, middle, low, ones], axis=0)
        return sums + lax.dot_general(
            rows, table, (((1,), (1,)), ((), ())), preferred_element_type=jnp.float32
        )

    sums = lax.fori_loop(
        0, tracers // chunk, step, jnp.zeros((4 * props, total_bins), jnp.float32)
    )
    total = sums[:props] + sums[props : 2 * props] + sums[2 * props : 3 * props]
    mean_ref[...] = total / jnp.maximum(sums[3 * props :], 1.0)


def bin_means(base, holder, voxel, attributes, blocks):
    props, tracers = attributes.shape
    chunk = 1024 if tracers % 1024 == 0 else tracers
    vmem = pl.BlockSpec(memory_space=pltpu.VMEM)
    return pl.pallas_call(
        functools.partial(bin_kernel, blocks=blocks, chunk=chunk),
        out_shape=jax.ShapeDtypeStruct((props, blocks * BINS), jnp.float32),
        in_specs=[pl.BlockSpec(memory_space=pltpu.SMEM), vmem, vmem, vmem],
        out_specs=vmem,
        compiler_params=pltpu.CompilerParams(vmem_limit_bytes=32 * 1024 * 1024),
        cost_estimate=pl.CostEstimate(
            flops=2 * 32 * tracers * blocks * BINS, bytes_accessed=40 * tracers, transcendentals=0
        ),
    )(base.reshape(1), holder.reshape(1, tracers), voxel.reshape(1, tracers), attributes)


def swap_groups(x):
    row = lax.broadcasted_iota(jnp.int32, x.shape, 1)
    group = lax.broadcasted_iota(jnp.int32, x.shape, 2) // BS
    for bit in (1, 2, 4):
        row_set = (row & bit) != 0
        group_set = (group & bit) != 0
        from_above = pltpu.roll(pltpu.roll(x, 8 - bit, 1), BS * bit, 2)
        from_below = pltpu.roll(pltpu.roll(x, bit, 1), 8 * BS - BS * bit, 2)
        x = jnp.where(
            row_set == group_set, x, jnp.where(group_set, from_above, from_below)
        )
    return x


def pick_kernel(index_ref, from_ref, to_ref, sems):
    count = to_ref.shape[0]

    def copy_of(i):
        return pltpu.make_async_copy(from_ref.at[index_ref[i]], to_ref.at[i], sems.at[i])

    for i in range(count):
        copy_of(i).start()
    for i in range(count):
        copy_of(i).wait()


def pick(index, array):
    return pl.pallas_call(
        pick_kernel,
        out_shape=jax.ShapeDtypeStruct(index.shape + array.shape[1:], array.dtype),
        in_specs=[
            pl.BlockSpec(memory_space=pltpu.SMEM),
            pl.BlockSpec(memory_space=pltpu.VMEM),
        ],
        out_specs=pl.BlockSpec(memory_space=pl.ANY),
        scratch_shapes=[pltpu.SemaphoreType.DMA(index.shape)],
        compiler_params=pltpu.CompilerParams(vmem_limit_bytes=32 * 1024 * 1024),
    )(index, array)


def unpack_kernel(slot_ref, recv_ref, mix_ref, state_ref, heat_ref, held, sems):
    places = LY * LZ
    copies = []
    for r in range(places):
        copies.append(
            pltpu.make_async_copy(
                recv_ref.at[slot_ref[r]], held.at[r // LZ, :, r % LZ, :], sems.at[r]
            )
        )
        copies[-1].start()
    for copy in copies:
        copy.wait()
    spread = (
        lax.broadcasted_iota(jnp.int32, (32, 128), 0)
        == lax.broadcasted_iota(jnp.int32, (32, 128), 1) // 4
    ).astype(jnp.float32)
    wide_mix = jnp.dot(
        mix_ref[...], spread, precision=lax.Precision.HIGHEST, preferred_element_type=jnp.float32
    )
    for y in range(LY):
        rows = slice(y * BS, (y + 1) * BS)
        for field in range(4):
            part = swap_groups(held[y, field * 32 : (field + 1) * 32])
            state_ref[field, :, rows, :] = part.reshape(BS, BS, 128)
        heat = swap_groups(held[y, 128:160]).reshape(BS, BS, 128)
        heat_ref[:, rows, :] = heat
        drag = swap_groups(held[y, 160:192]).reshape(BS, BS, 128)
        for layer in range(4):
            piece = wide_mix[layer * 8 + y * 4 : layer * 8 + y * 4 + 4]
            piece = jnp.concatenate(
                [jnp.broadcast_to(piece[j : j + 1], (4, 128)) for j in range(4)], axis=0
            )
            at = slice(layer * 4, layer * 4 + 4)
            state_ref[4, at, rows, :] = drag[at] * jnp.exp(
                HEAT_FACTOR * (0.5 - heat[at]) + piece[None]
            )


def unpack(slots, received, mixture):
    grid_shape = (BS, LY * BS, LZ * BS)
    vmem = pl.BlockSpec(memory_space=pltpu.VMEM)
    return pl.pallas_call(
        unpack_kernel,
        out_shape=(
            jax.ShapeDtypeStruct((5,) + grid_shape, jnp.float32),
            jax.ShapeDtypeStruct(grid_shape, jnp.float32),
        ),
        in_specs=[
            pl.BlockSpec(memory_space=pltpu.SMEM),
            pl.BlockSpec(memory_space=pl.ANY),
            vmem,
        ],
        out_specs=(vmem, vmem),
        scratch_shapes=[
            pltpu.VMEM((LY, 192, LZ, 128), jnp.float32),
            pltpu.SemaphoreType.DMA((LY * LZ,)),
        ],
        compiler_params=pltpu.CompilerParams(vmem_limit_bytes=32 * 1024 * 1024),
    )(slots, received, mixture)


def sweep_kernel(
    state_ref, heat_ref, velocity_ref, pressure_ref,
    pad_0, pad_1, pad_2, edge_out, edge_in, send_sems, recv_sems,
    *, wide_count, narrow_count,
):
    wide, narrow = lax.axis_index("wide"), lax.axis_index("narrow")
    nx, ny, nz = heat_ref.shape
    exists = (wide > 0, wide < wide_count - 1, narrow > 0, narrow < narrow_count - 1)
    partner = ((wide - 1, narrow), (wide + 1, narrow), (wide, narrow - 1), (wide, narrow + 1))
    barrier = pltpu.get_barrier_semaphore()
    pads = (pad_0, pad_1, pad_2)
    for pad in pads:
        fields = pad.shape[0]
        for x in (0, nx + 1):
            pad[:, x] = jnp.zeros((fields, ny, nz), jnp.float32)
    edge_in[...] = jnp.zeros(edge_in.shape, jnp.float32)
    for side in range(4):

        @pl.when(exists[side])
        def _(side=side):
            pl.semaphore_signal(barrier, inc=1, device_id=partner[side], device_id_type=MESH)

    pad_0[:, 1 : nx + 1] = state_ref[...]
    pl.semaphore_wait(barrier, sum(there.astype(jnp.int32) for there in exists))

    row = lax.broadcasted_iota(jnp.int32, (ny, nz), 0)
    column = lax.broadcasted_iota(jnp.int32, (ny, nz), 1)

    def copy_of(turn, side):
        pad = pads[turn]
        fields = pad.shape[0]
        if side == 0:
            source, target = pad.at[:, 1], pad.at[:, nx + 1]
        elif side == 1:
            source, target = pad.at[:, nx], pad.at[:, 0]
        else:
            source = edge_out.at[turn, side - 2, pl.ds(0, fields)]
            target = edge_in.at[turn, 3 - side, pl.ds(0, fields)]
        return pltpu.make_async_remote_copy(
            src_ref=source,
            dst_ref=target,
            send_sem=send_sems.at[turn, side],
            recv_sem=recv_sems.at[turn, side ^ 1],
            device_id=partner[side],
            device_id_type=MESH,
        )

    def arrival_of(turn, side):
        pad = pads[turn]
        fields = pad.shape[0]
        if side < 2:
            target = pad.at[:, 0 if side == 0 else nx + 1]
        else:
            target = edge_in.at[turn, side - 2, pl.ds(0, fields)]
        return pltpu.make_async_remote_copy(
            src_ref=target,
            dst_ref=target,
            send_sem=send_sems.at[turn, side],
            recv_sem=recv_sems.at[turn, side],
            device_id=partner[side],
            device_id_type=MESH,
        )

    for turn in range(SWEEPS):
        pad = pads[turn]
        for side in range(2):

            @pl.when(exists[side])
            def _(side=side):
                copy_of(turn, side).start()

        for field in range(pad.shape[0]):
            edge_out[turn, 0, field] = pad[field, 1 : nx + 1, 0, :]
            edge_out[turn, 1, field] = pad[field, 1 : nx + 1, ny - 1, :]
        for side in range(2, 4):

            @pl.when(exists[side])
            def _(side=side):
                copy_of(turn, side).start()

        for side in range(4):

            @pl.when(exists[side])
            def _(side=side):
                arrival_of(turn, side).wait_recv()

        def slab(x, carry, turn=turn, pad=pad):
            def around(ref, edges, field):
                centre = ref[field, x + 1]
                low = edges[0, field, pl.ds(x, 1), :]
                high = edges[1, field, pl.ds(x, 1), :]
                return (
                    centre,
                    ref[field, x + 2],
                    ref[field, x],
                    jnp.where(row == ny - 1, high, pltpu.roll(centre, ny - 1, 0)),
                    jnp.where(row == 0, low, pltpu.roll(centre, 1, 0)),
                    jnp.where(column == nz - 1, 0.0, pltpu.roll(centre, nz - 1, 1)),
                    jnp.where(column == 0, 0.0, pltpu.roll(centre, 1, 1)),
                )

            eta = around(pad_0, edge_in.at[0], 4)
            face = [0.5 * (eta[0] + eta[m]) for m in range(1, 7)]
            diagonal = face[0]
            for m in range(1, 6):
                diagonal = diagonal + face[m]
            scale = RELAX_WEIGHT / diagonal
            press = around(pad, edge_in.at[turn], 3)
            divergence = None
            for component in range(3):
                speed = around(pad, edge_in.at[turn], component)
                residual = face[0] * (speed[1] - speed[0])
                for m in range(1, 6):
                    residual = residual + face[m] * (speed[m + 1] - speed[0])
                up, down = 2 * component + 1, 2 * component + 2
                residual = residual - 0.5 * (press[up] - press[down])
                if component == 2:
                    residual = residual + DENSITY_FACTOR * heat_ref[x]
                moved = speed[0] + residual * scale
                if turn < SWEEPS - 1:
                    pads[turn + 1][component, x + 1] = moved
                else:
                    velocity_ref[component, x] = moved
                flux = 0.5 * (speed[up] - speed[down])
                divergence = flux if divergence is None else divergence + flux
            moved = press[0] - PRESSURE_WEIGHT * eta[0] * divergence
            if turn < SWEEPS - 1:
                pads[turn + 1][3, x + 1] = moved
            else:
                pressure_ref[x] = moved
            return carry

        lax.fori_loop(0, nx, slab, 0)

    for turn in range(SWEEPS):
        for side in range(4):

            @pl.when(exists[side])
            def _(turn=turn, side=side):
                copy_of(turn, side).wait_send()


def sweeps(state, heat):
    nx, ny, nz = heat.shape
    vmem = pl.BlockSpec(memory_space=pltpu.VMEM)
    return pl.pallas_call(
        functools.partial(
            sweep_kernel,
            wide_count=lax.axis_size("wide"),
            narrow_count=lax.axis_size("narrow"),
        ),
        out_shape=(
            jax.ShapeDtypeStruct((3, nx, ny, nz), jnp.float32),
            jax.ShapeDtypeStruct((nx, ny, nz), jnp.float32),
        ),
        in_specs=[vmem, vmem],
        out_specs=(vmem, vmem),
        scratch_shapes=[
            pltpu.VMEM((5, nx + 2, ny, nz), jnp.float32),
            pltpu.VMEM((4, nx + 2, ny, nz), jnp.float32),
            pltpu.VMEM((4, nx + 2, ny, nz), jnp.float32),
            pltpu.VMEM((SWEEPS, 2, 5, nx, nz), jnp.float32),
            pltpu.VMEM((SWEEPS, 2, 5, nx, nz), jnp.float32),
            pltpu.SemaphoreType.DMA((SWEEPS, 4)),
            pltpu.SemaphoreType.DMA((SWEEPS, 4)),
        ],
        compiler_params=pltpu.CompilerParams(
            collective_id=1, has_side_effects=True, vmem_limit_bytes=32 * 1024 * 1024
        ),
    )(state, heat)


def per_device(
    tile_flow_speed,
    tile_stress_mean,
    tile_heat_state,
    tile_drag_coefficient,
    marker_attributes,
    marker_holding_tile,
    marker_voxel_number,
    prior_slot_of_tile,
):
    wide_count = lax.axis_size("wide")
    narrow_count = lax.axis_size("narrow")
    my_index = lax.axis_index("wide") * narrow_count + lax.axis_index("narrow")
    blocks = prior_slot_of_tile.shape[0]
    props = marker_attributes.shape[0]
    block_for = choose_blocks(prior_slot_of_tile)
    stacked = jnp.concatenate(
        [
            tile_flow_speed.reshape(blocks, 96, 128),
            tile_stress_mean.reshape(blocks, 32, 128),
            tile_heat_state.reshape(blocks, 32, 128),
            tile_drag_coefficient.reshape(blocks, 32, 128),
        ],
        axis=1,
    )
    outgoing = pick(block_for, stacked)
    outgoing, marker_attributes = lax.optimization_barrier((outgoing, marker_attributes))
    received = lax.all_to_all(
        outgoing, ("wide", "narrow"), split_axis=0, concat_axis=0, tiled=True
    )
    means = bin_means(
        my_index * blocks, marker_holding_tile, marker_voxel_number, marker_attributes, blocks
    )
    by_block = means.reshape(props, blocks, BINS).transpose(1, 0, 2).reshape(blocks, 4, 128)
    received_means = exchange(pick(block_for, by_block))
    source_dev = prior_slot_of_tile // blocks
    arrived = pick(source_dev, received_means).reshape(LX, LY, LZ, props, 4, 4, 4)
    bin_mean_attributes = arrived.transpose(3, 0, 4, 1, 5, 2, 6)
    bin_mean_attributes = bin_mean_attributes.reshape(props, LX * 4, LY * 4, LZ * 4)
    mixture = MIX_WEIGHTS[0] * bin_mean_attributes[0]
    for index_p in range(1, props):
        mixture = mixture + MIX_WEIGHTS[index_p] * bin_mean_attributes[index_p]
    state, heat = unpack(source_dev, received, mixture.reshape(LY * BS, LZ * 4))
    velocity, pressure = sweeps(state, heat)
    return (velocity, pressure, heat, bin_mean_attributes)


def solution(mesh):
    in_specs = (
        P(("wide", "narrow"), None, None),
        P(("wide", "narrow"), None),
        P(("wide", "narrow"), None),
        P(("wide", "narrow"), None),
        P(None, ("wide", "narrow")),
        P(("wide", "narrow")),
        P(("wide", "narrow")),
        P(("wide", "narrow")),
    )
    out_specs = (
        P(None, "wide", "narrow", None),
        P("wide", "narrow", None),
        P("wide", "narrow", None),
        P(None, "wide", "narrow", None),
    )
    return jax.shard_map(
        per_device, mesh=mesh, in_specs=in_specs, out_specs=out_specs, check_vma=False
    )
```

```python
import functools

import jax
import jax.numpy as jnp
from jax import lax
from jax.experimental import pallas as pl
from jax.experimental.pallas import tpu as pltpu
from jax.sharding import PartitionSpec as P

BS = 16
LX = 1
LY = 2
LZ = 8
SWEEPS = 3
BINS = 64

MIX_WEIGHTS = (0.3, -0.25, 0.2, -0.15, 0.35, -0.3, 0.25, -0.2)
RELAX_WEIGHT = 0.7
PRESSURE_WEIGHT = 0.3
HEAT_FACTOR = 2.0
DENSITY_FACTOR = 4.0
MESH = pl.DeviceIdType.MESH


def choose_kernel(
    mine_ref, block_ref, table, send_sems, recv_sems, *, wide_count, narrow_count, blocks
):
    count = wide_count * narrow_count
    me = lax.axis_index("wide") * narrow_count + lax.axis_index("narrow")

    def place(step):
        return lax.rem(me + step, count)

    def coordinates(step):
        other = place(step)
        return (lax.div(other, narrow_count), lax.rem(other, narrow_count))

    barrier = pltpu.get_barrier_semaphore()

    def greet(step, carry):
        pl.semaphore_signal(barrier, inc=1, device_id=coordinates(step), device_id_type=MESH)
        return carry

    lax.fori_loop(1, count, greet, 0)
    pl.semaphore_wait(barrier, count - 1)

    def copy_of(step, target):
        return pltpu.make_async_remote_copy(
            src_ref=mine_ref.at[0],
            dst_ref=table.at[target],
            send_sem=send_sems.at[step],
            recv_sem=recv_sems.at[step],
            device_id=coordinates(step),
            device_id_type=MESH,
        )

    def send(step, carry):
        copy_of(step, me).start()
        return carry

    lax.fori_loop(1, count, send, 0)
    table[me] = mine_ref[0]

    def finish(step, carry):
        copy_of(step, place(count - step)).wait_recv()
        copy_of(step, me).wait_send()
        return carry

    lax.fori_loop(1, count, finish, 0)
    local_old = table[...] - me * blocks
    is_mine = (local_old >= 0) & (local_old < blocks)
    block_ref[...] = jnp.sum(jnp.where(is_mine, local_old, 0), axis=2)


def choose_blocks(prior_slots):
    wide_count, narrow_count = lax.axis_size("wide"), lax.axis_size("narrow")
    count, blocks = wide_count * narrow_count, prior_slots.shape[0]
    padded = jnp.pad(prior_slots, (0, 128 - blocks), constant_values=-1).reshape(1, 1, 128)
    vmem = pl.BlockSpec(memory_space=pltpu.VMEM)
    return pl.pallas_call(
        functools.partial(
            choose_kernel, wide_count=wide_count, narrow_count=narrow_count, blocks=blocks
        ),
        out_shape=jax.ShapeDtypeStruct((count, 1), jnp.int32),
        in_specs=[vmem],
        out_specs=vmem,
        scratch_shapes=[
            pltpu.VMEM((count, 1, 128), jnp.int32),
            pltpu.SemaphoreType.DMA((count,)),
            pltpu.SemaphoreType.DMA((count,)),
        ],
        compiler_params=pltpu.CompilerParams(collective_id=2, has_side_effects=True),
    )(padded).reshape(count)


def exchange_kernel(
    send_ref, out_ref, landed, send_sems, recv_sems, *, wide_count, narrow_count
):
    count = wide_count * narrow_count
    me = lax.axis_index("wide") * narrow_count + lax.axis_index("narrow")

    def place(step):
        return lax.rem(me + step, count)

    def coordinates(step):
        other = place(step)
        return (lax.div(other, narrow_count), lax.rem(other, narrow_count))

    barrier = pltpu.get_barrier_semaphore()

    def greet(step, carry):
        pl.semaphore_signal(barrier, inc=1, device_id=coordinates(step), device_id_type=MESH)
        return carry

    lax.fori_loop(1, count, greet, 0)
    pl.semaphore_wait(barrier, count - 1)

    def copy_of(step, target):
        return pltpu.make_async_remote_copy(
            src_ref=send_ref.at[place(step)],
            dst_ref=landed.at[target],
            send_sem=send_sems.at[step],
            recv_sem=recv_sems.at[step],
            device_id=coordinates(step),
            device_id_type=MESH,
        )

    def send(step, carry):
        copy_of(step, me).start()
        return carry

    lax.fori_loop(1, count, send, 0)
    landed[me] = send_ref[me]

    def finish(step, carry):
        copy_of(step, place(count - step)).wait_recv()
        copy_of(step, me).wait_send()
        return carry

    lax.fori_loop(1, count, finish, 0)
    out_ref[...] = landed[...]


def exchange(entries):
    wide_count, narrow_count = lax.axis_size("wide"), lax.axis_size("narrow")
    count = wide_count * narrow_count
    vmem = pl.BlockSpec(memory_space=pltpu.VMEM)
    return pl.pallas_call(
        functools.partial(exchange_kernel, wide_count=wide_count, narrow_count=narrow_count),
        out_shape=jax.ShapeDtypeStruct(entries.shape, entries.dtype),
        in_specs=[vmem],
        out_specs=vmem,
        scratch_shapes=[
            pltpu.VMEM(entries.shape, entries.dtype),
            pltpu.SemaphoreType.DMA((count,)),
            pltpu.SemaphoreType.DMA((count,)),
        ],
        compiler_params=pltpu.CompilerParams(
            collective_id=3, has_side_effects=True, vmem_limit_bytes=32 * 1024 * 1024
        ),
    )(entries)


def bin_kernel(base_ref, holder_ref, voxel_ref, attr_ref, mean_ref, *, blocks, chunk):
    props, tracers = attr_ref.shape
    total_bins = blocks * BINS
    base = base_ref[0]
    bin_ids = lax.broadcasted_iota(jnp.int32, (total_bins, chunk), 0)

    def step(turn, sums):
        at = pl.ds(pl.multiple_of(turn * chunk, chunk), chunk)
        voxel = voxel_ref[:, at]
        key = (
            (holder_ref[:, at] - base) * BINS
            + (voxel >> 10) * 16
            + ((voxel >> 6) & 3) * 4
            + ((voxel >> 2) & 3)
        )
        table = jnp.where(bin_ids == key, 1.0, 0.0).astype(jnp.bfloat16)
        values = attr_ref[:, at]
        high = values.astype(jnp.bfloat16)
        rest = values - high.astype(jnp.float32)
        middle = rest.astype(jnp.bfloat16)
        low = (rest - middle.astype(jnp.float32)).astype(jnp.bfloat16)
        ones = jnp.ones((props, chunk), jnp.bfloat16)
        rows = jnp.concatenate([high, middle, low, ones], axis=0)
        return sums + lax.dot_general(
            rows, table, (((1,), (1,)), ((), ())), preferred_element_type=jnp.float32
        )

    sums = lax.fori_loop(
        0, tracers // chunk, step, jnp.zeros((4 * props, total_bins), jnp.float32)
    )
    total = sums[:props] + sums[props : 2 * props] + sums[2 * props : 3 * props]
    mean_ref[...] = total / jnp.maximum(sums[3 * props :], 1.0)


def bin_means(base, holder, voxel, attributes, blocks):
    props, tracers = attributes.shape
    chunk = 1024 if tracers % 1024 == 0 else tracers
    vmem = pl.BlockSpec(memory_space=pltpu.VMEM)
    return pl.pallas_call(
        functools.partial(bin_kernel, blocks=blocks, chunk=chunk),
        out_shape=jax.ShapeDtypeStruct((props, blocks * BINS), jnp.float32),
        in_specs=[pl.BlockSpec(memory_space=pltpu.SMEM), vmem, vmem, vmem],
        out_specs=vmem,
        compiler_params=pltpu.CompilerParams(vmem_limit_bytes=32 * 1024 * 1024),
        cost_estimate=pl.CostEstimate(
            flops=2 * 32 * tracers * blocks * BINS, bytes_accessed=40 * tracers, transcendentals=0
        ),
    )(base.reshape(1), holder.reshape(1, tracers), voxel.reshape(1, tracers), attributes)


def swap_groups(x):
    row = lax.broadcasted_iota(jnp.int32, x.shape, 1)
    group = lax.broadcasted_iota(jnp.int32, x.shape, 2) // BS
    for bit in (1, 2, 4):
        row_set = (row & bit) != 0
        group_set = (group & bit) != 0
        from_above = pltpu.roll(pltpu.roll(x, 8 - bit, 1), BS * bit, 2)
        from_below = pltpu.roll(pltpu.roll(x, bit, 1), 8 * BS - BS * bit, 2)
        x = jnp.where(
            row_set == group_set, x, jnp.where(group_set, from_above, from_below)
        )
    return x


def pick_kernel(index_ref, from_ref, to_ref, sems):
    count = to_ref.shape[0]

    def copy_of(i):
        return pltpu.make_async_copy(from_ref.at[index_ref[i]], to_ref.at[i], sems.at[i])

    for i in range(count):
        copy_of(i).start()
    for i in range(count):
        copy_of(i).wait()


def pick(index, array):
    return pl.pallas_call(
        pick_kernel,
        out_shape=jax.ShapeDtypeStruct(index.shape + array.shape[1:], array.dtype),
        in_specs=[
            pl.BlockSpec(memory_space=pltpu.SMEM),
            pl.BlockSpec(memory_space=pltpu.VMEM),
        ],
        out_specs=pl.BlockSpec(memory_space=pl.ANY),
        scratch_shapes=[pltpu.SemaphoreType.DMA(index.shape)],
        compiler_params=pltpu.CompilerParams(vmem_limit_bytes=32 * 1024 * 1024),
    )(index, array)


def unpack_kernel(slot_ref, recv_ref, mix_ref, state_ref, heat_ref, held, sems):
    places = LY * LZ
    copies = []
    for r in range(places):
        copies.append(
            pltpu.make_async_copy(
                recv_ref.at[slot_ref[r]], held.at[r // LZ, :, r % LZ, :], sems.at[r]
            )
        )
        copies[-1].start()
    for copy in copies:
        copy.wait()
    spread = (
        lax.broadcasted_iota(jnp.int32, (32, 128), 0)
        == lax.broadcasted_iota(jnp.int32, (32, 128), 1) // 4
    ).astype(jnp.float32)
    wide_mix = jnp.dot(
        mix_ref[...], spread, precision=lax.Precision.HIGHEST, preferred_element_type=jnp.float32
    )
    for y in range(LY):
        rows = slice(y * BS, (y + 1) * BS)
        for field in range(4):
            part = swap_groups(held[y, field * 32 : (field + 1) * 32])
            state_ref[field, :, rows, :] = part.reshape(BS, BS, 128)
        heat = swap_groups(held[y, 128:160]).reshape(BS, BS, 128)
        heat_ref[:, rows, :] = heat
        drag = swap_groups(held[y, 160:192]).reshape(BS, BS, 128)
        for layer in range(4):
            piece = wide_mix[layer * 8 + y * 4 : layer * 8 + y * 4 + 4]
            piece = jnp.concatenate(
                [jnp.broadcast_to(piece[j : j + 1], (4, 128)) for j in range(4)], axis=0
            )
            at = slice(layer * 4, layer * 4 + 4)
            state_ref[4, at, rows, :] = drag[at] * jnp.exp(
                HEAT_FACTOR * (0.5 - heat[at]) + piece[None]
            )


def unpack(slots, received, mixture):
    grid_shape = (BS, LY * BS, LZ * BS)
    vmem = pl.BlockSpec(memory_space=pltpu.VMEM)
    return pl.pallas_call(
        unpack_kernel,
        out_shape=(
            jax.ShapeDtypeStruct((5,) + grid_shape, jnp.float32),
            jax.ShapeDtypeStruct(grid_shape, jnp.float32),
        ),
        in_specs=[
            pl.BlockSpec(memory_space=pltpu.SMEM),
            pl.BlockSpec(memory_space=pl.ANY),
            vmem,
        ],
        out_specs=(vmem, vmem),
        scratch_shapes=[
            pltpu.VMEM((LY, 192, LZ, 128), jnp.float32),
            pltpu.SemaphoreType.DMA((LY * LZ,)),
        ],
        compiler_params=pltpu.CompilerParams(vmem_limit_bytes=32 * 1024 * 1024),
    )(slots, received, mixture)


def sweep_kernel(
    state_ref, heat_ref, velocity_ref, pressure_ref,
    pad_0, pad_1, pad_2, edge_out, edge_in, send_sems, recv_sems,
    *, wide_count, narrow_count,
):
    wide, narrow = lax.axis_index("wide"), lax.axis_index("narrow")
    nx, ny, nz = heat_ref.shape
    exists = (wide > 0, wide < wide_count - 1, narrow > 0, narrow < narrow_count - 1)
    partner = ((wide - 1, narrow), (wide + 1, narrow), (wide, narrow - 1), (wide, narrow + 1))
    barrier = pltpu.get_barrier_semaphore()
    pads = (pad_0, pad_1, pad_2)
    for pad in pads:
        fields = pad.shape[0]
        for x in (0, nx + 1):
            pad[:, x] = jnp.zeros((fields, ny, nz), jnp.float32)
    edge_in[...] = jnp.zeros(edge_in.shape, jnp.float32)
    for side in range(4):

        @pl.when(exists[side])
        def _(side=side):
            pl.semaphore_signal(barrier, inc=1, device_id=partner[side], device_id_type=MESH)

    pad_0[:, 1 : nx + 1] = state_ref[...]
    pl.semaphore_wait(barrier, sum(there.astype(jnp.int32) for there in exists))

    row = lax.broadcasted_iota(jnp.int32, (ny, nz), 0)
    column = lax.broadcasted_iota(jnp.int32, (ny, nz), 1)

    def copy_of(turn, side):
        pad = pads[turn]
        fields = pad.shape[0]
        if side == 0:
            source, target = pad.at[:, 1], pad.at[:, nx + 1]
        elif side == 1:
            source, target = pad.at[:, nx], pad.at[:, 0]
        else:
            source = edge_out.at[turn, side - 2, pl.ds(0, fields)]
            target = edge_in.at[turn, 3 - side, pl.ds(0, fields)]
        return pltpu.make_async_remote_copy(
            src_ref=source,
            dst_ref=target,
            send_sem=send_sems.at[turn, side],
            recv_sem=recv_sems.at[turn, side ^ 1],
            device_id=partner[side],
            device_id_type=MESH,
        )

    def arrival_of(turn, side):
        pad = pads[turn]
        fields = pad.shape[0]
        if side < 2:
            target = pad.at[:, 0 if side == 0 else nx + 1]
        else:
            target = edge_in.at[turn, side - 2, pl.ds(0, fields)]
        return pltpu.make_async_remote_copy(
            src_ref=target,
            dst_ref=target,
            send_sem=send_sems.at[turn, side],
            recv_sem=recv_sems.at[turn, side],
            device_id=partner[side],
            device_id_type=MESH,
        )

    for turn in range(SWEEPS):
        pad = pads[turn]
        for side in range(2):

            @pl.when(exists[side])
            def _(side=side):
                copy_of(turn, side).start()

        for field in range(pad.shape[0]):
            edge_out[turn, 0, field] = pad[field, 1 : nx + 1, 0, :]
            edge_out[turn, 1, field] = pad[field, 1 : nx + 1, ny - 1, :]
        for side in range(2, 4):

            @pl.when(exists[side])
            def _(side=side):
                copy_of(turn, side).start()

        for side in range(4):

            @pl.when(exists[side])
            def _(side=side):
                arrival_of(turn, side).wait_recv()

        def slab(x, carry, turn=turn, pad=pad):
            def around(ref, edges, field):
                centre = ref[field, x + 1]
                low = edges[0, field, pl.ds(x, 1), :]
                high = edges[1, field, pl.ds(x, 1), :]
                return (
                    centre,
                    ref[field, x + 2],
                    ref[field, x],
                    jnp.where(row == ny - 1, high, pltpu.roll(centre, ny - 1, 0)),
                    jnp.where(row == 0, low, pltpu.roll(centre, 1, 0)),
                    jnp.where(column == nz - 1, 0.0, pltpu.roll(centre, nz - 1, 1)),
                    jnp.where(column == 0, 0.0, pltpu.roll(centre, 1, 1)),
                )

            eta = around(pad_0, edge_in.at[0], 4)
            face = [0.5 * (eta[0] + eta[m]) for m in range(1, 7)]
            diagonal = face[0]
            for m in range(1, 6):
                diagonal = diagonal + face[m]
            scale = RELAX_WEIGHT / diagonal
            press = around(pad, edge_in.at[turn], 3)
            divergence = None
            for component in range(3):
                speed = around(pad, edge_in.at[turn], component)
                residual = face[0] * (speed[1] - speed[0])
                for m in range(1, 6):
                    residual = residual + face[m] * (speed[m + 1] - speed[0])
                up, down = 2 * component + 1, 2 * component + 2
                residual = residual - 0.5 * (press[up] - press[down])
                if component == 2:
                    residual = residual + DENSITY_FACTOR * heat_ref[x]
                moved = speed[0] + residual * scale
                if turn < SWEEPS - 1:
                    pads[turn + 1][component, x + 1] = moved
                else:
                    velocity_ref[component, x] = moved
                flux = 0.5 * (speed[up] - speed[down])
                divergence = flux if divergence is None else divergence + flux
            moved = press[0] - PRESSURE_WEIGHT * eta[0] * divergence
            if turn < SWEEPS - 1:
                pads[turn + 1][3, x + 1] = moved
            else:
                pressure_ref[x] = moved
            return carry

        lax.fori_loop(0, nx, slab, 0, unroll=2)

    for turn in range(SWEEPS):
        for side in range(4):

            @pl.when(exists[side])
            def _(turn=turn, side=side):
                copy_of(turn, side).wait_send()


def sweeps(state, heat):
    nx, ny, nz = heat.shape
    vmem = pl.BlockSpec(memory_space=pltpu.VMEM)
    return pl.pallas_call(
        functools.partial(
            sweep_kernel,
            wide_count=lax.axis_size("wide"),
            narrow_count=lax.axis_size("narrow"),
        ),
        out_shape=(
            jax.ShapeDtypeStruct((3, nx, ny, nz), jnp.float32),
            jax.ShapeDtypeStruct((nx, ny, nz), jnp.float32),
        ),
        in_specs=[vmem, vmem],
        out_specs=(vmem, vmem),
        scratch_shapes=[
            pltpu.VMEM((5, nx + 2, ny, nz), jnp.float32),
            pltpu.VMEM((4, nx + 2, ny, nz), jnp.float32),
            pltpu.VMEM((4, nx + 2, ny, nz), jnp.float32),
            pltpu.VMEM((SWEEPS, 2, 5, nx, nz), jnp.float32),
            pltpu.VMEM((SWEEPS, 2, 5, nx, nz), jnp.float32),
            pltpu.SemaphoreType.DMA((SWEEPS, 4)),
            pltpu.SemaphoreType.DMA((SWEEPS, 4)),
        ],
        compiler_params=pltpu.CompilerParams(
            collective_id=1, has_side_effects=True, vmem_limit_bytes=32 * 1024 * 1024
        ),
    )(state, heat)


def per_device(
    tile_flow_speed,
    tile_stress_mean,
    tile_heat_state,
    tile_drag_coefficient,
    marker_attributes,
    marker_holding_tile,
    marker_voxel_number,
    prior_slot_of_tile,
):
    wide_count = lax.axis_size("wide")
    narrow_count = lax.axis_size("narrow")
    my_index = lax.axis_index("wide") * narrow_count + lax.axis_index("narrow")
    blocks = prior_slot_of_tile.shape[0]
    props = marker_attributes.shape[0]
    block_for = choose_blocks(prior_slot_of_tile)
    stacked = jnp.concatenate(
        [
            tile_flow_speed.reshape(blocks, 96, 128),
            tile_stress_mean.reshape(blocks, 32, 128),
            tile_heat_state.reshape(blocks, 32, 128),
            tile_drag_coefficient.reshape(blocks, 32, 128),
        ],
        axis=1,
    )
    outgoing = pick(block_for, stacked)
    means = bin_means(
        my_index * blocks, marker_holding_tile, marker_voxel_number, marker_attributes, blocks
    )
    by_block = means.reshape(props, blocks, BINS).transpose(1, 0, 2).reshape(blocks, 4, 128)
    received_means = exchange(pick(block_for, by_block))
    outgoing, received_means = lax.optimization_barrier((outgoing, received_means))
    received = lax.all_to_all(
        outgoing, ("wide", "narrow"), split_axis=0, concat_axis=0, tiled=True
    )
    source_dev = prior_slot_of_tile // blocks
    arrived = pick(source_dev, received_means).reshape(LX, LY, LZ, props, 4, 4, 4)
    bin_mean_attributes = arrived.transpose(3, 0, 4, 1, 5, 2, 6)
    bin_mean_attributes = bin_mean_attributes.reshape(props, LX * 4, LY * 4, LZ * 4)
    mixture = MIX_WEIGHTS[0] * bin_mean_attributes[0]
    for index_p in range(1, props):
        mixture = mixture + MIX_WEIGHTS[index_p] * bin_mean_attributes[index_p]
    state, heat = unpack(source_dev, received, mixture.reshape(LY * BS, LZ * 4))
    velocity, pressure = sweeps(state, heat)
    return (velocity, pressure, heat, bin_mean_attributes)


def solution(mesh):
    in_specs = (
        P(("wide", "narrow"), None, None),
        P(("wide", "narrow"), None),
        P(("wide", "narrow"), None),
        P(("wide", "narrow"), None),
        P(None, ("wide", "narrow")),
        P(("wide", "narrow")),
        P(("wide", "narrow")),
        P(("wide", "narrow")),
    )
    out_specs = (
        P(None, "wide", "narrow", None),
        P("wide", "narrow", None),
        P("wide", "narrow", None),
        P(None, "wide", "narrow", None),
    )
    return jax.shard_map(
        per_device, mesh=mesh, in_specs=in_specs, out_specs=out_specs, check_vma=False
    )
```
